32 devices in a mesh: groups: 2 (over y), neuron: 16 (over z, x, core).
Axes of the slice: x: 2, y: 2, z: 4, core: 2. Of those that a mesh axis runs over, the one named last changes fastest.
Arguments:
- tokens: bfloat16 [512, 12288], P(('groups', 'neuron')), parts along dimension 0, may hold values from -6 to 6
- active: int32 [128, 3], P(('groups', 'neuron')), parts along dimension 0, may hold values from 0 to 31, as said below
- ln_gain: bfloat16 [12288], replicated, may hold values from 0.099609375 to 1.8984375
- ln_bias: bfloat16 [12288], replicated, may hold values from -3 to 3
- w_in: bfloat16 [12288, 4096], P(None, 'neuron'), may hold values from -0.0546875 to 0.0546875
- b_in: bfloat16 [4096], P('neuron'), may hold values from -3 to 3
- w_out: bfloat16 [4096, 12288], P('neuron'), may hold values from -0.3125 to 0.3125
- b_out: bfloat16 [12288], replicated, may hold values from -2 to 2
Outputs:
- mixed: bfloat16 [512, 12288], P(('groups', 'neuron')), parts along dimension 0
The draws below stay inside these ranges and needn't reach their ends.
There are 2 independent parts, one for each index of `groups`. The reference program is written for one: setup_inputs(seed, part) draws one part's arguments, and reference() takes and returns one part's arrays. A program takes and returns all parts, laid end to end along the dimension named above; an argument that names none is the same for every part. Nothing has to cross between parts.
Inputs may be any that keep to these rules, and one draw needn't show every extreme that they name: Each row names 3 distinct blocks. Block b lies with device b // 2 of the neuron axis, and the 4 requests held by one device never have active blocks lying with the same device.
All inputs are finite; a program needn't handle non-finite values.
Results may differ from the reference program's by a relative error of at most 0.0051.
Values may be sent and summed in bfloat16 or wider, within the bound.
No kernel may reach another device: no remote copies, remote signals or barrier semaphores. Data moves between devices by JAX's collectives and lax.ppermute only.
A program may use at most 128 MiB of HBM per device.

```python
import jax
import jax.numpy as jnp
from jax import lax

D = 12288
BLK = 128
BLK_DEV = 2
NODES = 4
REQ_DEV = 4
BLOCKS = 32
FF = 4096
ACTIVE = 3
ROWS = 256
N_NEURON = 16


def draw_active(key, part):
    key = jax.random.fold_in(key, 11)
    heat_key, order_key, jitter_key = jax.random.split(key, 3)
    share_count = N_NEURON // REQ_DEV
    block_heat = jax.random.randint(heat_key, (BLOCKS,), 0, 4)
    orders = jax.vmap(lambda one_key: jax.random.permutation(one_key, N_NEURON))(jax.random.split(order_key, N_NEURON))
    request_devices = orders.reshape(N_NEURON, REQ_DEV, share_count)
    candidates = request_devices[..., None] * BLK_DEV + jnp.arange(BLK_DEV, dtype=jnp.int32)
    candidates = candidates.reshape(N_NEURON * REQ_DEV, share_count * BLK_DEV).astype(jnp.int32)
    jitter = jax.random.randint(jitter_key, candidates.shape, 0, 64)
    ranking = (block_heat[candidates] * 48 + jitter) * (share_count * BLK_DEV) + jnp.arange(share_count * BLK_DEV, dtype=jnp.int32)
    _, picked = lax.top_k(ranking, ACTIVE)
    return jnp.take_along_axis(candidates, picked, axis=1).astype(jnp.int32)


def block_levels(own_key, extent, pieces, smallest, high):
    def one(position, shards_of):
        heights = jax.random.uniform(jax.random.fold_in(jax.random.fold_in(own_key, 6), position), (shards_of,), jnp.float32, smallest / len(pieces), high / len(pieces))
        return jnp.repeat(jnp.exp(heights), extent[position] // shards_of).reshape((-1,) + (1,) * (len(extent) - position - 1))

    loudness = one(*pieces[0])
    for cut in pieces[1:]:
        loudness = loudness * one(*cut)
    return loudness


def scatter_about(rng, dims, scale, bound, pieces=(), held_as=jnp.bfloat16):
    values = scale * jax.random.normal(rng, dims, jnp.float32)
    if pieces:
        values = values * block_levels(rng, dims, pieces, -0.22, 0.18)
    return jnp.clip(values, -bound, bound).astype(held_as)


def setup_inputs(seed: int = 0, part: int = 0) -> dict:
    splits = jax.random.split(jax.random.key(seed), 9)
    part_splits = jax.random.split(jax.random.fold_in(splits[8], part), 9)
    return {
        "tokens": scatter_about(part_splits[0], (ROWS, D), 1.0, 6.0, ((0, 16),)),
        "active": draw_active(jax.random.fold_in(jax.random.fold_in(splits[8], part), 71), part),
        "ln_gain": jnp.clip(1.0 + 0.18 * jax.random.normal(splits[2], (D,), jnp.float32), 0.099609375, 1.8984375).astype(jnp.bfloat16),
        "ln_bias": scatter_about(splits[3], (D,), 0.5, 3.0),
        "w_in": scatter_about(splits[4], (D, FF), D ** -0.5, 0.0546875, ((1, 16),)),
        "b_in": scatter_about(splits[5], (FF,), 0.5, 3.0, ((0, 16),)),
        "w_out": scatter_about(splits[6], (FF, D), (ACTIVE * BLK) ** -0.5, 0.3125, ((0, 16),)),
        "b_out": scatter_about(splits[7], (D,), 0.3, 2.0),
    }


epsilon = 1e-05

def layer_norm(tokens, ln_gain, ln_bias):
    widened = tokens.astype(jnp.float32)
    row_mean = lax.optimization_barrier(jnp.mean(widened, axis=1, keepdims=True))
    centred = widened - row_mean
    row_var = lax.optimization_barrier(jnp.mean(centred * centred, axis=1, keepdims=True))
    scaled = centred * lax.rsqrt(row_var + epsilon)
    return (scaled * ln_gain.astype(jnp.float32) + ln_bias.astype(jnp.float32)).astype(jnp.bfloat16)

def reference(tokens, active, ln_gain, ln_bias, w_in, b_in, w_out, b_out):
    normed = layer_norm(tokens, ln_gain, ln_bias)
    block_ids = jnp.arange(BLOCKS, dtype=jnp.int32)
    opened = lax.optimization_barrier(jnp.sum((active[:, :, None] == block_ids[None, None, :]).astype(jnp.int32), axis=1))
    row_open = jnp.repeat(opened, NODES, axis=0)
    group_width = BLK_DEV * BLK

    def add_group(group_index, summed):
        unit_start = (group_index * group_width).astype(jnp.int32)
        block_start = (group_index * BLK_DEV).astype(jnp.int32)
        w_slice = lax.dynamic_slice_in_dim(w_in, unit_start, group_width, 1)
        b_slice = lax.dynamic_slice_in_dim(b_in, unit_start, group_width, 0)
        out_slice = lax.dynamic_slice_in_dim(w_out, unit_start, group_width, 0)
        mask_slice = lax.dynamic_slice_in_dim(row_open, block_start, BLK_DEV, 1)
        unit_mask = jnp.repeat(mask_slice, BLK, axis=1).astype(jnp.float32)
        preact = jnp.dot(normed, w_slice, preferred_element_type=jnp.float32) + b_slice.astype(jnp.float32)
        hidden = (jnp.maximum(preact, 0.0) * unit_mask).astype(jnp.bfloat16)
        partial_value = jnp.dot(hidden, out_slice, preferred_element_type=jnp.float32).astype(jnp.bfloat16)
        partial_value = lax.optimization_barrier(partial_value)
        return summed + partial_value.astype(jnp.float32)
    summed = lax.fori_loop(0, N_NEURON, add_group, jnp.zeros((ROWS, D), jnp.float32))
    mixed = tokens.astype(jnp.float32) + summed + b_out.astype(jnp.float32)
    return mixed.astype(jnp.bfloat16)
```

```python
import functools

import jax
import jax.numpy as jnp
from jax import lax
from jax.experimental import pallas as pl
from jax.experimental.pallas import tpu as pltpu
from jax.sharding import PartitionSpec as P

BLK = 128
LANES = 128
SUB = 8
VMEM_LIMIT = 56 * 1024 * 1024

epsilon = 1e-05


def route_matrix(active_ref, row_count, col_count, per_device, nodes, transposed):
    requests, active = active_ref.shape
    shape = (col_count, row_count) if transposed else (row_count, col_count)
    slot = lax.broadcasted_iota(jnp.int32, shape, 1 if transposed else 0)
    item = lax.broadcasted_iota(jnp.int32, shape, 0 if transposed else 1)
    per_half = requests * nodes
    device, inner = slot // SUB, slot % SUB
    half, request, node = item // per_half, (item % per_half) // nodes, item % nodes
    aligned = inner == half * nodes + node
    touched = jnp.zeros(shape, jnp.bool_)
    for r in range(requests):
        for a in range(active):
            touched = touched | ((request == r) & (device == active_ref[r, a] // per_device))
    return jnp.where(touched & aligned, 1.0, 0.0)


def send_kernel(active_ref, tokens_ref, gain_ref, bias_ref, out_ref, *, per_device, nodes):
    rows, features = tokens_ref.shape
    half = features // 2
    slots = out_ref.shape[0]
    requests, active = active_ref.shape
    total = jnp.zeros((rows, LANES), jnp.float32)
    for j in range(0, features, LANES):
        total += tokens_ref[:, j : j + LANES].astype(jnp.float32)
    mean = jnp.sum(total, axis=1, keepdims=True) / features
    total = jnp.zeros((rows, LANES), jnp.float32)
    for j in range(0, features, LANES):
        centred = tokens_ref[:, j : j + LANES].astype(jnp.float32) - mean
        total += centred * centred
    scale = lax.rsqrt(jnp.sum(total, axis=1, keepdims=True) / features + epsilon)
    route = route_matrix(active_ref, slots, 2 * rows, per_device, nodes, False).astype(jnp.bfloat16)

    def normed(start, width):
        centred = tokens_ref[:, pl.ds(start, width)].astype(jnp.float32) - mean
        gain = gain_ref[:, pl.ds(start, width)].astype(jnp.float32)
        bias = bias_ref[:, pl.ds(start, width)].astype(jnp.float32)
        return (centred * scale * gain + bias).astype(jnp.bfloat16)

    width = 512
    for j in range(0, half, width):
        both = jnp.concatenate([normed(j, width), normed(half + j, width)], axis=0)
        out_ref[:, j : j + width] = jnp.dot(route, both, preferred_element_type=jnp.float32).astype(jnp.bfloat16)
    device = lax.broadcasted_iota(jnp.int32, (slots, LANES), 0) // SUB
    lane = lax.broadcasted_iota(jnp.int32, (slots, LANES), 1)
    flags = jnp.zeros((slots, LANES), jnp.bool_)
    for r in range(requests):
        for a in range(active):
            block = active_ref[r, a]
            flags = flags | ((device == block // per_device) & (lane == block % per_device))
    out_ref[:, half:] = jnp.where(flags, 1.0, 0.0).astype(jnp.bfloat16)


def neuron_kernel(x_ref, w_in_hbm, b_in_ref, w_out_hbm, out_ref, w_in, w_out, in_sem, out_sem, *, nodes, parts):
    slots = x_ref.shape[0]
    features, units = w_in.shape
    half = features // 2
    depth, width = half // parts, half // parts
    in_copies, out_copies = [], []
    for k in range(2 * parts):
        span = pl.ds(k * depth, depth)
        in_copies.append(pltpu.make_async_copy(w_in_hbm.at[span, :], w_in.at[span, :], in_sem.at[k]))
        in_copies[-1].start()
    for k in range(2 * parts):
        span = pl.ds(k * width, width)
        out_copies.append(pltpu.make_async_copy(w_out_hbm.at[:, span], w_out.at[:, span], out_sem.at[k]))
    for k in range(parts):
        out_copies[k].start()
        out_copies[parts + k].start()
    sums = []
    for h in range(2):
        total = jnp.zeros((slots, units), jnp.float32)
        for k in range(parts):
            in_copies[h * parts + k].wait()
            at = h * half + k * depth
            total += jnp.dot(
                x_ref[:, k * depth : (k + 1) * depth],
                w_in[at : at + depth, :],
                preferred_element_type=jnp.float32,
            )
        sums.append(total)
    first, second = sums
    upper = lax.broadcasted_iota(jnp.int32, (slots, 1), 0) % SUB < nodes
    preact = jnp.where(
        upper,
        first + pltpu.roll(second, slots - nodes, 0),
        second + pltpu.roll(first, nodes, 0),
    ) + b_in_ref[...].astype(jnp.float32)
    hidden = []
    for b in range(units // BLK):
        flag = x_ref[:, half : half + LANES].astype(jnp.float32)[:, b : b + 1]
        hidden.append(jnp.maximum(preact[:, b * BLK : (b + 1) * BLK], 0.0) * flag)
    hidden = jnp.concatenate(hidden, axis=1).astype(jnp.bfloat16)
    for k in range(parts):
        out_copies[k].wait()
        out_copies[parts + k].wait()
        at = k * width
        lo = jnp.dot(hidden, w_out[:, at : at + width], preferred_element_type=jnp.float32)
        hi = jnp.dot(hidden, w_out[:, half + at : half + at + width], preferred_element_type=jnp.float32)
        out_ref[:, at : at + width] = jnp.where(upper, lo, hi).astype(jnp.bfloat16)


def finish_kernel(active_ref, returned_ref, tokens_ref, b_out_ref, out_ref, *, per_device, nodes):
    rows, features = tokens_ref.shape
    half = features // 2
    slots = returned_ref.shape[0]
    route = route_matrix(active_ref, slots, 2 * rows, per_device, nodes, True).astype(jnp.bfloat16)
    width = 512
    for j in range(0, half, width):
        both = jnp.dot(route, returned_ref[:, j : j + width], preferred_element_type=jnp.float32)
        for h in range(2):
            at = h * half + j
            mixed = (
                tokens_ref[:, at : at + width].astype(jnp.float32)
                + both[h * rows : (h + 1) * rows]
                + b_out_ref[:, at : at + width].astype(jnp.float32)
            )
            out_ref[:, at : at + width] = mixed.astype(jnp.bfloat16)


def body(tokens, active, ln_gain, ln_bias, w_in, b_in, w_out, b_out):
    rows, features = tokens.shape
    requests = active.shape[0]
    nodes = rows // requests
    units = w_in.shape[1]
    half = features // 2
    device_count = lax.axis_size("neuron")
    per_device = units // BLK
    slots = device_count * SUB
    params = pltpu.CompilerParams(vmem_limit_bytes=VMEM_LIMIT)
    smem = pl.BlockSpec(memory_space=pltpu.SMEM)
    vmem = pl.BlockSpec(memory_space=pltpu.VMEM)
    outgoing = pl.pallas_call(
        functools.partial(send_kernel, per_device=per_device, nodes=nodes),
        out_shape=jax.ShapeDtypeStruct((slots, half + LANES), jnp.bfloat16),
        in_specs=[smem, vmem, vmem, vmem],
        out_specs=vmem,
        compiler_params=params,
    )(active, tokens, ln_gain[None], ln_bias[None])
    arrived = lax.all_to_all(
        outgoing.reshape(device_count, SUB, half + LANES), "neuron", split_axis=0, concat_axis=0, tiled=True
    ).reshape(slots, half + LANES)
    parts = 4
    block = min(slots, 16 * SUB)
    hbm = pl.BlockSpec(memory_space=pl.ANY)
    partial_value = pl.pallas_call(
        functools.partial(neuron_kernel, nodes=nodes, parts=parts),
        out_shape=jax.ShapeDtypeStruct((slots, half), jnp.bfloat16),
        grid=(slots // block,),
        in_specs=[
            pl.BlockSpec((block, half + LANES), lambda i: (i, 0)),
            hbm,
            pl.BlockSpec((1, units), lambda i: (0, 0)),
            hbm,
        ],
        out_specs=pl.BlockSpec((block, half), lambda i: (i, 0)),
        scratch_shapes=[
            pltpu.VMEM((features, units), jnp.bfloat16),
            pltpu.VMEM((units, features), jnp.bfloat16),
            pltpu.SemaphoreType.DMA((2 * parts,)),
            pltpu.SemaphoreType.DMA((2 * parts,)),
        ],
        compiler_params=params,
    )(arrived, w_in, b_in[None], w_out)
    returned = lax.all_to_all(
        partial_value.reshape(device_count, SUB, half), "neuron", split_axis=0, concat_axis=0, tiled=True
    ).reshape(slots, half)
    return pl.pallas_call(
        functools.partial(finish_kernel, per_device=per_device, nodes=nodes),
        out_shape=jax.ShapeDtypeStruct((rows, features), jnp.bfloat16),
        in_specs=[smem, vmem, vmem, vmem],
        out_specs=vmem,
        compiler_params=params,
    )(active, returned, tokens, b_out[None])


def solution(mesh):
    placed = (
        P(("groups", "neuron"), None),
        P(("groups", "neuron"), None),
        P(),
        P(),
        P(None, "neuron"),
        P("neuron"),
        P("neuron", None),
        P(),
    )
    return jax.shard_map(
        body, mesh=mesh, in_specs=placed, out_specs=P(("groups", "neuron"), None), check_vma=False
    )
```

```python
import functools

import jax
import jax.numpy as jnp
from jax import lax
from jax.experimental import pallas as pl
from jax.experimental.pallas import tpu as pltpu
from jax.sharding import PartitionSpec as P

BLK = 128
LANES = 128
SUB = 8
WIDTH = 512
MIB = 1024 * 1024
SELECT_COST = 10_000_000_000

epsilon = 1e-05


def iota(shape, axis):
    return lax.broadcasted_iota(jnp.int32, shape, axis)


def touches(ids, device, per_device, active):
    owner = (ids.astype(jnp.int32) + (per_device - 1)) // per_device - 1
    touched = jnp.zeros(device.shape, jnp.bool_)
    for a in range(active):
        touched = touched | (owner[:, a : a + 1] == device)
    return touched


def spread_matrix(ids, first_device, device_count, per_device, active):
    shape = (ids.shape[0], device_count * SUB)
    wanted = iota(shape, 1) % SUB == iota(shape, 0) % SUB
    touched = touches(ids, first_device + iota(shape, 1) // SUB, per_device, active)
    return jnp.where(touched & wanted, 1.0, 0.0)


def near_matrix(ids, chips, per_device, active):
    shape = (ids.shape[0], chips * SUB)
    wanted = iota(shape, 1) % SUB == iota(shape, 0) % SUB
    me = lax.axis_index("neuron")
    device = 2 * (me // 2 ^ iota(shape, 1) // SUB) + me % 2
    return jnp.where(touches(ids, device, per_device, active) & wanted, 1.0, 0.0)


def half_start(half_count):
    return lax.axis_index("neuron") // half_count * half_count


def norm_kernel(active_ref, tokens_ref, gain_ref, bias_ref, out_ref, *, nodes):
    rows, features = tokens_ref.shape
    half = features // 2
    packed = 2 * rows
    requests, active = active_ref.shape
    total = jnp.zeros((rows, LANES), jnp.float32)
    for j in range(0, features, LANES):
        total += tokens_ref[:, j : j + LANES].astype(jnp.float32)
    mean = jnp.sum(total, axis=1, keepdims=True) / features
    total = jnp.zeros((rows, LANES), jnp.float32)
    for j in range(0, features, LANES):
        centred = tokens_ref[:, j : j + LANES].astype(jnp.float32) - mean
        total += centred * centred
    scale = lax.rsqrt(jnp.sum(total, axis=1, keepdims=True) / features + epsilon)
    shape = (packed, packed)
    slot, item = iota(shape, 0), iota(shape, 1)
    source = (slot % SUB // nodes) * rows + slot // SUB * nodes + slot % nodes
    pack = jnp.where(item == source, 1.0, 0.0).astype(jnp.bfloat16)

    def normed(start):
        centred = tokens_ref[:, start : start + WIDTH].astype(jnp.float32) - mean
        gain = gain_ref[start : start + WIDTH].astype(jnp.float32).reshape(1, WIDTH)
        bias = bias_ref[start : start + WIDTH].astype(jnp.float32).reshape(1, WIDTH)
        return (centred * scale * gain + bias).astype(jnp.bfloat16)

    for j in range(0, half, WIDTH):
        both = jnp.concatenate([normed(j), normed(half + j)], axis=0)
        out_ref[:, j : j + WIDTH] = jnp.dot(pack, both, preferred_element_type=jnp.float32).astype(jnp.bfloat16)
    request, lane = iota((packed, LANES), 0) // SUB, iota((packed, LANES), 1)
    ids = jnp.zeros((packed, LANES), jnp.int32)
    for r in range(requests):
        for a in range(active):
            ids = jnp.where((request == r) & (lane == a), active_ref[r, a] + 1, ids)
    out_ref[:, half:] = ids.astype(jnp.float32).astype(jnp.bfloat16)


def select_kernel(packed_ref, *refs, half_count, per_device, active):
    out_ref = refs[-1]
    total = packed_ref.shape[1]
    half = total - LANES
    ids = packed_ref[:, half:].astype(jnp.float32)
    spread = spread_matrix(ids, half_start(half_count), half_count, per_device, active)
    chosen = spread.T.astype(jnp.bfloat16)
    for j in list(range(0, half, WIDTH)) + [half]:
        span = slice(j, min(j + WIDTH, total) if j < half else total)
        out_ref[:, span] = jnp.dot(chosen, packed_ref[:, span], preferred_element_type=jnp.float32).astype(jnp.bfloat16)


def select_near_kernel(own_ref, mate_ref, *out_refs, per_device, active):
    total = own_ref.shape[1]
    half = total - LANES
    chips = len(out_refs)
    for s, packed_ref in enumerate((own_ref, mate_ref)):
        ids = packed_ref[:, half:].astype(jnp.float32)
        chosen = near_matrix(ids, chips, per_device, active).T.astype(jnp.bfloat16)
        for j in list(range(0, half, WIDTH)) + [half]:
            span = slice(j, min(j + WIDTH, total) if j < half else total)
            rows = jnp.dot(chosen, packed_ref[:, span], preferred_element_type=jnp.float32)
            for k, out_ref in enumerate(out_refs):
                out_ref[s * SUB : (s + 1) * SUB, span] = rows[k * SUB : (k + 1) * SUB].astype(jnp.bfloat16)


def neuron_kernel(*refs, nodes, chips):
    near_refs, refs = refs[:chips], refs[chips:]
    far_ref, w_in_ref, b_in_ref, w_out_ref = refs[:4]
    near_out_refs, far_out_ref, x_ref = refs[4:-2], refs[-2], refs[-1]
    slots = x_ref.shape[0]
    features, units = w_in_ref.shape
    half = features // 2
    per_device = units // BLK
    depth = half // 4
    for k, near_ref in enumerate(near_refs):
        x_ref[2 * SUB * k : 2 * SUB * (k + 1), :] = near_ref[...]
    near_rows = 2 * SUB * chips
    x_ref[near_rows:, :] = far_ref[...]
    sums = []
    for h in range(2):
        total = jnp.zeros((slots, units), jnp.float32)
        for at in range(0, half, depth):
            total += jnp.dot(
                x_ref[:, at : at + depth],
                w_in_ref[h * half + at : h * half + at + depth, :],
                preferred_element_type=jnp.float32,
            )
        sums.append(total)
    first, second = sums
    upper = iota((slots, 1), 0) % SUB < nodes
    preact = jnp.where(
        upper,
        first + pltpu.roll(second, slots - nodes, 0),
        second + pltpu.roll(first, nodes, 0),
    ) + b_in_ref[...].astype(jnp.float32).reshape(1, units)
    ids = x_ref[:, half : half + LANES].astype(jnp.float32).astype(jnp.int32)
    own = lax.axis_index("neuron") * per_device + 1
    hidden = []
    for b in range(per_device):
        flag = jnp.max(jnp.where(ids == own + b, 1.0, 0.0), axis=1, keepdims=True)
        hidden.append(jnp.maximum(preact[:, b * BLK : (b + 1) * BLK], 0.0) * flag)
    hidden = jnp.concatenate(hidden, axis=1).astype(jnp.bfloat16)
    for at in range(0, half, depth):
        lo = jnp.dot(hidden, w_out_ref[:, at : at + depth], preferred_element_type=jnp.float32)
        hi = jnp.dot(hidden, w_out_ref[:, half + at : half + at + depth], preferred_element_type=jnp.float32)
        both = jnp.where(upper, lo, hi).astype(jnp.bfloat16)
        for k, near_out_ref in enumerate(near_out_refs):
            near_out_ref[:, at : at + depth] = both[2 * SUB * k : 2 * SUB * (k + 1)]
        far_out_ref[:, at : at + depth] = both[near_rows:]


def gather_kernel(packed_ref, returned_ref, *refs, half_count, per_device, active):
    half = returned_ref.shape[1]
    count = len(refs) // 2
    out_ref = refs[count]
    for part_ref, copy_ref in zip(refs[:count], refs[count + 1 :], strict=True):
        copy_ref[...] = part_ref[...]
    ids = packed_ref[:, half:].astype(jnp.float32)
    spread = spread_matrix(ids, half_start(half_count), half_count, per_device, active).astype(jnp.bfloat16)
    for j in range(0, half, WIDTH):
        part = jnp.dot(spread, returned_ref[:, j : j + WIDTH], preferred_element_type=jnp.float32)
        out_ref[:, j : j + WIDTH] = part.astype(jnp.bfloat16)


def gather_near_kernel(own_ref, mate_ref, *refs, per_device, active):
    back_refs, out_refs = refs[:-2], refs[-2:]
    half = back_refs[0].shape[1]
    chips = len(back_refs)
    for s, packed_ref in enumerate((own_ref, mate_ref)):
        spread = near_matrix(packed_ref[:, half:].astype(jnp.float32), chips, per_device, active).astype(jnp.bfloat16)
        for j in range(0, half, WIDTH):
            back = jnp.concatenate([ref[s * SUB : (s + 1) * SUB, j : j + WIDTH] for ref in back_refs], axis=0)
            part = jnp.dot(spread, back, preferred_element_type=jnp.float32)
            out_refs[s][:, j : j + WIDTH] = part.astype(jnp.bfloat16)


def finish_kernel(near_ref, mate_ref, far_ref, tokens_ref, b_out_ref, out_ref, *, nodes):
    rows, features = tokens_ref.shape
    half = features // 2
    shape = (2 * rows, 2 * rows)
    item, slot = iota(shape, 0), iota(shape, 1)
    source = item % rows // nodes * SUB + item // rows * nodes + item % nodes
    unpack = jnp.where(slot == source, 1.0, 0.0).astype(jnp.bfloat16)
    for j in range(0, half, WIDTH):
        both = jnp.zeros((2 * rows, WIDTH), jnp.float32)
        for ref in (near_ref, mate_ref, far_ref):
            both += jnp.dot(unpack, ref[:, j : j + WIDTH], preferred_element_type=jnp.float32)
        for h in range(2):
            at = h * half + j
            mixed = (
                tokens_ref[:, at : at + WIDTH].astype(jnp.float32)
                + both[h * rows : (h + 1) * rows]
                + b_out_ref[at : at + WIDTH].astype(jnp.float32).reshape(1, WIDTH)
            )
            out_ref[:, at : at + WIDTH] = mixed.astype(jnp.bfloat16)


def body(tokens, active, ln_gain, ln_bias, w_in, b_in, w_out, b_out):
    rows, features = tokens.shape
    requests, active_count = active.shape
    nodes = rows // requests
    units = w_in.shape[1]
    half = features // 2
    device_count = lax.axis_size("neuron")
    half_count = device_count // 2
    per_device = units // BLK
    packed = requests * SUB
    slots = half_count * SUB
    smem = pl.BlockSpec(memory_space=pltpu.SMEM)
    vmem = pl.BlockSpec(memory_space=pltpu.VMEM)
    hbm = pl.BlockSpec(memory_space=pl.ANY)
    chips = half_count // 2
    halves = [list(range(half_count)), list(range(half_count, device_count))]
    routing = dict(per_device=per_device, active=active_count)

    def call(kernel, shapes, in_specs, *operands, scratch=(), cost=0, limit=0):
        size = 2 * sum(rows * columns for rows, columns in shapes) + sum(x.size * 2 for x in operands)
        size += sum(2 * rows * columns for rows, columns in scratch)
        return pl.pallas_call(
            kernel,
            out_shape=[jax.ShapeDtypeStruct(shape, jnp.bfloat16) for shape in shapes],
            in_specs=in_specs,
            out_specs=[vmem] * len(shapes),
            scratch_shapes=[pltpu.VMEM(shape, jnp.bfloat16) for shape in scratch],
            compiler_params=pltpu.CompilerParams(vmem_limit_bytes=max(size + 8 * MIB, limit)),
            cost_estimate=pl.CostEstimate(flops=cost, bytes_accessed=size, transcendentals=0),
        )(*operands)

    def swap(x, partner):
        return lax.ppermute(x, "neuron", [(i, partner(i)) for i in range(device_count)])

    def across(x):
        return swap(x, lambda i: (i + half_count) % device_count)

    def mate_of(x):
        return swap(x, lambda i: i ^ 1)

    def to_chips(xs):
        return [xs[0]] + [swap(x, lambda i, k=k: i ^ 2 * k) for k, x in enumerate(xs) if k]

    def exchange(x):
        width = x.shape[1]
        return lax.all_to_all(
            x.reshape(half_count, SUB, width), "neuron", 0, 0, axis_index_groups=halves, tiled=True
        ).reshape(slots, width)

    [own] = call(
        functools.partial(norm_kernel, nodes=nodes),
        [(packed, half + LANES)],
        [smem, vmem, vmem, vmem],
        active, tokens, ln_gain, ln_bias,
        limit=56 * MIB,
    )
    other = across(own)
    mate = mate_of(own)
    near_slots = call(
        functools.partial(select_near_kernel, **routing),
        [(2 * SUB, half + LANES)] * chips,
        [vmem] * 2,
        own, mate,
    )
    near_rows = to_chips(near_slots)
    [far_slots] = call(
        functools.partial(select_kernel, half_count=half_count, **routing),
        [(slots, half + LANES)],
        [vmem] + [hbm] * (chips - 1),
        other, *near_rows[1:],
        cost=SELECT_COST,
    )
    far_rows = exchange(far_slots)
    *near_parts, far_part = call(
        functools.partial(neuron_kernel, nodes=nodes, chips=chips),
        [(2 * SUB, half)] * chips + [(slots, half)],
        [vmem] * (chips + 4),
        *near_rows, far_rows, w_in, b_in, w_out,
        scratch=[(2 * slots, half + LANES)],
    )
    far_back = exchange(far_part)
    gathered, *near_sent = call(
        functools.partial(gather_kernel, half_count=half_count, **routing),
        [(packed, half)] + [(2 * SUB, half)] * (chips - 1),
        [vmem] * (1 + chips),
        other, far_back, *near_parts[1:],
    )
    far_sum = across(gathered)
    near_own, near_mate = call(
        functools.partial(gather_near_kernel, **routing),
        [(packed, half)] * 2,
        [vmem] * (2 + chips),
        own, mate, *to_chips([near_parts[0], *near_sent]),
    )
    [mixed] = call(
        functools.partial(finish_kernel, nodes=nodes),
        [(rows, features)],
        [vmem] * 5,
        near_own, mate_of(near_mate), far_sum, tokens, b_out,
    )
    return mixed


def solution(mesh):
    placed = (
        P(("groups", "neuron"), None),
        P(("groups", "neuron"), None),
        P(),
        P(),
        P(None, "neuron"),
        P("neuron"),
        P("neuron", None),
        P(),
    )
    return jax.shard_map(
        body, mesh=mesh, in_specs=placed, out_specs=P(("groups", "neuron"), None), check_vma=False
    )
```

```python
import functools

import jax
import jax.numpy as jnp
from jax import lax
from jax.experimental import pallas as pl
from jax.experimental.pallas import tpu as pltpu
from jax.sharding import PartitionSpec as P

BLK = 128
LANES = 128
SUB = 8
WIDTH = 512
MIB = 1024 * 1024
SELECT_COST = 10_000_000_000
BACK_CHUNKS = 1

epsilon = 1e-05


def iota(shape, axis):
    return lax.broadcasted_iota(jnp.int32, shape, axis)


def touches(ids, device, per_device, active):
    owner = (ids.astype(jnp.int32) + (per_device - 1)) // per_device - 1
    touched = jnp.zeros(device.shape, jnp.bool_)
    for a in range(active):
        touched = touched | (owner[:, a : a + 1] == device)
    return touched


def route_matrix(ids, chips, per_device, active):
    shape = (ids.shape[0], chips * SUB)
    wanted = iota(shape, 1) % SUB == iota(shape, 0) % SUB
    me = lax.axis_index("neuron")
    device = 2 * (me // 2 ^ iota(shape, 1) // SUB) + me % 2
    return jnp.where(touches(ids, device, per_device, active) & wanted, 1.0, 0.0)


def norm_kernel(active_ref, tokens_ref, gain_ref, bias_ref, out_ref, *, nodes):
    rows, features = tokens_ref.shape
    half = features // 2
    packed = 2 * rows
    requests, active = active_ref.shape
    total = jnp.zeros((rows, LANES), jnp.float32)
    for j in range(0, features, LANES):
        total += tokens_ref[:, j : j + LANES].astype(jnp.float32)
    mean = jnp.sum(total, axis=1, keepdims=True) / features
    total = jnp.zeros((rows, LANES), jnp.float32)
    for j in range(0, features, LANES):
        centred = tokens_ref[:, j : j + LANES].astype(jnp.float32) - mean
        total += centred * centred
    scale = lax.rsqrt(jnp.sum(total, axis=1, keepdims=True) / features + epsilon)
    shape = (packed, packed)
    slot, item = iota(shape, 0), iota(shape, 1)
    source = (slot % SUB // nodes) * rows + slot // SUB * nodes + slot % nodes
    pack = jnp.where(item == source, 1.0, 0.0).astype(jnp.bfloat16)

    def normed(start):
        centred = tokens_ref[:, start : start + WIDTH].astype(jnp.float32) - mean
        gain = gain_ref[start : start + WIDTH].astype(jnp.float32).reshape(1, WIDTH)
        bias = bias_ref[start : start + WIDTH].astype(jnp.float32).reshape(1, WIDTH)
        return (centred * scale * gain + bias).astype(jnp.bfloat16)

    for j in range(0, half, WIDTH):
        both = jnp.concatenate([normed(j), normed(half + j)], axis=0)
        out_ref[:, j : j + WIDTH] = jnp.dot(pack, both, preferred_element_type=jnp.float32).astype(jnp.bfloat16)
    request, lane = iota((packed, LANES), 0) // SUB, iota((packed, LANES), 1)
    ids = jnp.zeros((packed, LANES), jnp.int32)
    for r in range(requests):
        for a in range(active):
            ids = jnp.where((request == r) & (lane == a), active_ref[r, a] + 1, ids)
    out_ref[:, half:] = ids.astype(jnp.float32).astype(jnp.bfloat16)


def select_kernel(own_ids_ref, mate_ids_ref, own_ref, mate_ref, *refs, chips, per_device, active):
    out_refs = refs[-chips:]
    total = own_ref.shape[1]
    for s, (ids_ref, packed_ref) in enumerate(((own_ids_ref, own_ref), (mate_ids_ref, mate_ref))):
        ids = ids_ref[:, ids_ref.shape[1] - LANES :].astype(jnp.float32)
        chosen = route_matrix(ids, chips, per_device, active).T.astype(jnp.bfloat16)
        for j in range(0, total, WIDTH):
            span = slice(j, min(j + WIDTH, total))
            rows = jnp.dot(chosen, packed_ref[:, span], preferred_element_type=jnp.float32)
            for k, out_ref in enumerate(out_refs):
                out_ref[s * SUB : (s + 1) * SUB, span] = rows[k * SUB : (k + 1) * SUB].astype(jnp.bfloat16)


def neuron_kernel(*refs, nodes, chips, chunks):
    x_ref = refs[-1]
    in_refs = [refs[:chips], refs[chips : 2 * chips]]
    at = 2 * chips
    w_in_ref, b_in_ref, w_out_ref = refs[at : at + 3]
    out_refs = [refs[at + 3 + i * chips : at + 3 + (i + 1) * chips] for i in range(1 + chunks)]
    slots = x_ref.shape[0]
    features, units = w_in_ref.shape
    half = features // 2
    per_device = units // BLK
    depth = half // 4
    chunk = half // chunks
    near_rows = 2 * SUB * chips
    for k in range(chips):
        here = slice(2 * SUB * k, 2 * SUB * (k + 1))
        x_ref[here, :] = in_refs[0][k][...]
        here = slice(near_rows + 2 * SUB * k, near_rows + 2 * SUB * (k + 1))
        x_ref[here, :] = in_refs[1][k][...]
    sums = []
    for h in range(2):
        total = jnp.zeros((slots, units), jnp.float32)
        for at in range(0, half, depth):
            total += jnp.dot(
                x_ref[:, at : at + depth],
                w_in_ref[h * half + at : h * half + at + depth, :],
                preferred_element_type=jnp.float32,
            )
        sums.append(total)
    first, second = sums
    upper = iota((slots, 1), 0) % SUB < nodes
    preact = jnp.where(
        upper,
        first + pltpu.roll(second, slots - nodes, 0),
        second + pltpu.roll(first, nodes, 0),
    ) + b_in_ref[...].astype(jnp.float32).reshape(1, units)
    ids = x_ref[:, half : half + LANES].astype(jnp.float32).astype(jnp.int32)
    own = lax.axis_index("neuron") * per_device + 1
    hidden = []
    for b in range(per_device):
        flag = jnp.max(jnp.where(ids == own + b, 1.0, 0.0), axis=1, keepdims=True)
        hidden.append(jnp.maximum(preact[:, b * BLK : (b + 1) * BLK], 0.0) * flag)
    hidden = jnp.concatenate(hidden, axis=1).astype(jnp.bfloat16)
    for at in range(0, half, depth):
        lo = jnp.dot(hidden, w_out_ref[:, at : at + depth], preferred_element_type=jnp.float32)
        hi = jnp.dot(hidden, w_out_ref[:, half + at : half + at + depth], preferred_element_type=jnp.float32)
        both = jnp.where(upper, lo, hi).astype(jnp.bfloat16)
        c, offset = at // chunk, at % chunk
        for k in range(chips):
            out_refs[0][k][:, at : at + depth] = both[2 * SUB * k : 2 * SUB * (k + 1)]
            far = both[near_rows + 2 * SUB * k : near_rows + 2 * SUB * (k + 1)]
            out_refs[1 + c][k][:, offset : offset + depth] = far


def gather_kernel(own_ref, mate_ref, *refs, chips, per_device, active):
    back_refs, out_refs = refs[:chips], refs[-2:]
    half = back_refs[0].shape[1]
    for s, ids_ref in enumerate((own_ref, mate_ref)):
        ids = ids_ref[:, ids_ref.shape[1] - LANES :].astype(jnp.float32)
        spread = route_matrix(ids, chips, per_device, active).astype(jnp.bfloat16)
        for j in range(0, half, WIDTH):
            back = jnp.concatenate([ref[s * SUB : (s + 1) * SUB, j : j + WIDTH] for ref in back_refs], axis=0)
            part = jnp.dot(spread, back, preferred_element_type=jnp.float32)
            out_refs[s][:, j : j + WIDTH] = part.astype(jnp.bfloat16)


def copy_kernel(*refs):
    count = len(refs) // 2
    for part_ref, copy_ref in zip(refs[:count], refs[count + 1 :], strict=True):
        copy_ref[...] = part_ref[...]


def finish_kernel(near_ref, mate_ref, *refs, nodes):
    far_refs, (tokens_ref, b_out_ref, out_ref) = refs[:-3], refs[-3:]
    rows, features = tokens_ref.shape
    half = features // 2
    shape = (2 * rows, 2 * rows)
    item, slot = iota(shape, 0), iota(shape, 1)
    source = item % rows // nodes * SUB + item // rows * nodes + item % nodes
    unpack = jnp.where(slot == source, 1.0, 0.0).astype(jnp.bfloat16)
    chunk = half // len(far_refs)
    for j in range(0, half, WIDTH):
        far = far_refs[j // chunk][:, j % chunk : j % chunk + WIDTH]
        both = jnp.zeros((2 * rows, WIDTH), jnp.float32)
        for part in (near_ref[:, j : j + WIDTH], mate_ref[:, j : j + WIDTH], far):
            both += jnp.dot(unpack, part, preferred_element_type=jnp.float32)
        for h in range(2):
            at = h * half + j
            mixed = (
                tokens_ref[:, at : at + WIDTH].astype(jnp.float32)
                + both[h * rows : (h + 1) * rows]
                + b_out_ref[at : at + WIDTH].astype(jnp.float32).reshape(1, WIDTH)
            )
            out_ref[:, at : at + WIDTH] = mixed.astype(jnp.bfloat16)


def body(tokens, active, ln_gain, ln_bias, w_in, b_in, w_out, b_out):
    rows, features = tokens.shape
    requests, active_count = active.shape
    nodes = rows // requests
    units = w_in.shape[1]
    half = features // 2
    device_count = lax.axis_size("neuron")
    half_count = device_count // 2
    per_device = units // BLK
    packed = requests * SUB
    smem = pl.BlockSpec(memory_space=pltpu.SMEM)
    vmem = pl.BlockSpec(memory_space=pltpu.VMEM)
    hbm = pl.BlockSpec(memory_space=pl.ANY)
    chips = half_count // 2
    routing = dict(chips=chips, per_device=per_device, active=active_count)
    back_chunk = half // BACK_CHUNKS

    def call(kernel, shapes, in_specs, *operands, scratch=(), cost=0, limit=0):
        size = 2 * sum(rows * columns for rows, columns in shapes) + sum(x.size * 2 for x in operands)
        size += sum(2 * rows * columns for rows, columns in scratch)
        return pl.pallas_call(
            kernel,
            out_shape=[jax.ShapeDtypeStruct(shape, jnp.bfloat16) for shape in shapes],
            in_specs=in_specs,
            out_specs=[vmem] * len(shapes),
            scratch_shapes=[pltpu.VMEM(shape, jnp.bfloat16) for shape in scratch],
            compiler_params=pltpu.CompilerParams(vmem_limit_bytes=max(size + 8 * MIB, limit)),
            cost_estimate=pl.CostEstimate(flops=cost, bytes_accessed=size, transcendentals=0),
        )(*operands)

    def after(x, *others):
        return pl.pallas_call(
            lambda *refs: None,
            out_shape=jax.ShapeDtypeStruct(x.shape, x.dtype),
            in_specs=[hbm] * (1 + len(others)),
            out_specs=hbm,
            input_output_aliases={0: 0},
            compiler_params=pltpu.CompilerParams(vmem_limit_bytes=MIB),
            cost_estimate=pl.CostEstimate(flops=0, bytes_accessed=0, transcendentals=0),
        )(x, *others)

    def swap(x, partner):
        return lax.ppermute(x, "neuron", [(i, partner(i)) for i in range(device_count)])

    def across(x):
        return swap(x, lambda i: (i + half_count) % device_count)

    def mate_of(x):
        return swap(x, lambda i: i ^ 1)

    def to_chips(xs):
        return [xs[0]] + [swap(x, lambda i, k=k: i ^ 2 * k) for k, x in enumerate(xs) if k]

    def select(ids, packed_rows, order, cost):
        return call(
            functools.partial(select_kernel, **routing),
            [(2 * SUB, packed_rows[0].shape[1])] * chips,
            [vmem] * 4 + [hbm] * len(order),
            *ids, *packed_rows, *order,
            cost=cost,
        )

    def gather(ids, parts, order=()):
        back = to_chips(parts)
        return call(
            functools.partial(gather_kernel, **routing),
            [(packed, back[0].shape[1])] * 2,
            [vmem] * (2 + chips) + [hbm] * len(order),
            *ids, *back, *order,
        )

    [own] = call(
        functools.partial(norm_kernel, nodes=nodes),
        [(packed, half + LANES)],
        [smem, vmem, vmem, vmem],
        active, tokens, ln_gain, ln_bias,
        limit=56 * MIB,
    )
    other = across(own)
    near_ids = own, mate_of(own)
    near_rows = to_chips(select(near_ids, near_ids, (), 0))
    other = after(other, *near_rows[1:])
    far_ids = other, mate_of(other)
    far_rows = to_chips(select(far_ids, far_ids, (), SELECT_COST))
    parts = call(
        functools.partial(neuron_kernel, nodes=nodes, chips=chips, chunks=BACK_CHUNKS),
        [(2 * SUB, half)] * chips + [(2 * SUB, back_chunk)] * (chips * BACK_CHUNKS),
        [vmem] * (2 * chips + 3),
        *near_rows, *far_rows, w_in, b_in, w_out,
        scratch=[(2 * half_count * SUB, half + LANES)],
    )
    near_parts = parts[:chips]
    totals, far_sums = [], []
    for c in range(BACK_CHUNKS):
        kept, passed = gather(far_ids, parts[(1 + c) * chips : (2 + c) * chips])
        total = kept.astype(jnp.float32) + mate_of(passed).astype(jnp.float32)
        totals.append(total.astype(jnp.bfloat16))
        far_sums.append(across(totals[-1]))
    near_sent = call(
        copy_kernel,
        [(2 * SUB, half)] * (chips - 1),
        [vmem] * (chips - 1) + [hbm],
        *near_parts[1:], totals[-1],
    )
    near_kept, near_passed = gather(near_ids, [near_parts[0], *near_sent])
    [mixed] = call(
        functools.partial(finish_kernel, nodes=nodes),
        [(rows, features)],
        [vmem] * (4 + BACK_CHUNKS),
        near_kept, mate_of(near_passed), *far_sums, tokens, b_out,
    )
    return mixed


def solution(mesh):
    placed = (
        P(("groups", "neuron"), None),
        P(("groups", "neuron"), None),
        P(),
        P(),
        P(None, "neuron"),
        P("neuron"),
        P("neuron", None),
        P(),
    )
    return jax.shard_map(
        body, mesh=mesh, in_specs=placed, out_specs=P(("groups", "neuron"), None), check_vma=False
    )
```

```python
import functools

import jax
import jax.numpy as jnp
from jax import lax
from jax.experimental import pallas as pl
from jax.experimental.pallas import tpu as pltpu
from jax.sharding import PartitionSpec as P

BLK = 128
LANES = 128
SUB = 8
WIDTH = 512
MIB = 1024 * 1024
SELECT_COST = 10_000_000_000

epsilon = 1e-05


def iota(shape, axis):
    return lax.broadcasted_iota(jnp.int32, shape, axis)


def touches(ids, device, per_device, active):
    owner = (ids.astype(jnp.int32) + (per_device - 1)) // per_device - 1
    touched = jnp.zeros(device.shape, jnp.bool_)
    for a in range(active):
        touched = touched | (owner[:, a : a + 1] == device)
    return touched


def route_matrix(ids, chips, per_device, active):
    shape = (ids.shape[0], chips * SUB)
    wanted = iota(shape, 1) % SUB == iota(shape, 0) % SUB
    me = lax.axis_index("neuron")
    device = 2 * (me // 2 ^ iota(shape, 1) // SUB) + me % 2
    return jnp.where(touches(ids, device, per_device, active) & wanted, 1.0, 0.0)


def norm_kernel(active_ref, tokens_ref, gain_ref, bias_ref, out_ref, *, nodes):
    rows, features = tokens_ref.shape
    half = features // 2
    packed = 2 * rows
    requests, active = active_ref.shape
    total = jnp.zeros((rows, LANES), jnp.float32)
    for j in range(0, features, LANES):
        total += tokens_ref[:, j : j + LANES].astype(jnp.float32)
    mean = jnp.sum(total, axis=1, keepdims=True) / features
    total = jnp.zeros((rows, LANES), jnp.float32)
    for j in range(0, features, LANES):
        centred = tokens_ref[:, j : j + LANES].astype(jnp.float32) - mean
        total += centred * centred
    scale = lax.rsqrt(jnp.sum(total, axis=1, keepdims=True) / features + epsilon)
    shape = (packed, packed)
    slot, item = iota(shape, 0), iota(shape, 1)
    source = (slot % SUB // nodes) * rows + slot // SUB * nodes + slot % nodes
    pack = jnp.where(item == source, 1.0, 0.0).astype(jnp.bfloat16)

    def normed(start):
        centred = tokens_ref[:, start : start + WIDTH].astype(jnp.float32) - mean
        gain = gain_ref[start : start + WIDTH].astype(jnp.float32).reshape(1, WIDTH)
        bias = bias_ref[start : start + WIDTH].astype(jnp.float32).reshape(1, WIDTH)
        return (centred * scale * gain + bias).astype(jnp.bfloat16)

    for j in range(0, half, WIDTH):
        both = jnp.concatenate([normed(j), normed(half + j)], axis=0)
        out_ref[:, j : j + WIDTH] = jnp.dot(pack, both, preferred_element_type=jnp.float32).astype(jnp.bfloat16)
    request, lane = iota((packed, LANES), 0) // SUB, iota((packed, LANES), 1)
    ids = jnp.zeros((packed, LANES), jnp.int32)
    for r in range(requests):
        for a in range(active):
            ids = jnp.where((request == r) & (lane == a), active_ref[r, a] + 1, ids)
    out_ref[:, half:] = ids.astype(jnp.float32).astype(jnp.bfloat16)


def select_kernel(own_ids_ref, mate_ids_ref, own_ref, mate_ref, *refs, chips, per_device, active):
    out_refs = refs[-chips:]
    total = own_ref.shape[1]
    for s, (ids_ref, packed_ref) in enumerate(((own_ids_ref, own_ref), (mate_ids_ref, mate_ref))):
        ids = ids_ref[:, ids_ref.shape[1] - LANES :].astype(jnp.float32)
        chosen = route_matrix(ids, chips, per_device, active).T.astype(jnp.bfloat16)
        for j in range(0, total, WIDTH):
            span = slice(j, min(j + WIDTH, total))
            rows = jnp.dot(chosen, packed_ref[:, span], preferred_element_type=jnp.float32)
            for k, out_ref in enumerate(out_refs):
                out_ref[s * SUB : (s + 1) * SUB, span] = rows[k * SUB : (k + 1) * SUB].astype(jnp.bfloat16)


def neuron_kernel(*refs, nodes, chips):
    x_ref = refs[-1]
    in_refs = [refs[:chips], refs[chips : 2 * chips]]
    at = 2 * chips
    w_in_ref, b_in_ref, w_out_ref = refs[at : at + 3]
    near_out_refs, far_out_refs = refs[at + 3 : at + 5], refs[at + 5 : -1]
    slots = x_ref.shape[0]
    features, units = w_in_ref.shape
    half = features // 2
    per_device = units // BLK
    depth = half // 4
    near_rows = 2 * SUB * chips
    for k in range(chips):
        here = slice(2 * SUB * k, 2 * SUB * (k + 1))
        x_ref[here, :] = in_refs[0][k][...]
        here = slice(near_rows + 2 * SUB * k, near_rows + 2 * SUB * (k + 1))
        x_ref[here, :] = in_refs[1][k][...]
    sums = []
    for h in range(2):
        total = jnp.zeros((slots, units), jnp.float32)
        for at in range(0, half, depth):
            total += jnp.dot(
                x_ref[:, at : at + depth],
                w_in_ref[h * half + at : h * half + at + depth, :],
                preferred_element_type=jnp.float32,
            )
        sums.append(total)
    first, second = sums
    upper = iota((slots, 1), 0) % SUB < nodes
    preact = jnp.where(
        upper,
        first + pltpu.roll(second, slots - nodes, 0),
        second + pltpu.roll(first, nodes, 0),
    ) + b_in_ref[...].astype(jnp.float32).reshape(1, units)
    ids = x_ref[:, half : half + LANES].astype(jnp.float32).astype(jnp.int32)
    own = lax.axis_index("neuron") * per_device + 1
    hidden = []
    for b in range(per_device):
        flag = jnp.max(jnp.where(ids == own + b, 1.0, 0.0), axis=1, keepdims=True)
        hidden.append(jnp.maximum(preact[:, b * BLK : (b + 1) * BLK], 0.0) * flag)
    hidden = jnp.concatenate(hidden, axis=1).astype(jnp.bfloat16)
    for at in range(0, half, depth):
        lo = jnp.dot(hidden, w_out_ref[:, at : at + depth], preferred_element_type=jnp.float32)
        hi = jnp.dot(hidden, w_out_ref[:, half + at : half + at + depth], preferred_element_type=jnp.float32)
        both = jnp.where(upper, lo, hi).astype(jnp.bfloat16)
        for k in range(chips):
            for s, near_out_ref in enumerate(near_out_refs):
                slot = both[(2 * k + s) * SUB : (2 * k + s + 1) * SUB]
                near_out_ref[k * SUB : (k + 1) * SUB, at : at + depth] = slot
            far = both[near_rows + 2 * SUB * k : near_rows + 2 * SUB * (k + 1)]
            far_out_refs[k][:, at : at + depth] = far


def gather_kernel(own_ref, mate_ref, *refs, chips, per_device, active):
    back_refs, out_refs = refs[:chips], refs[-2:]
    half = back_refs[0].shape[1]
    for s, ids_ref in enumerate((own_ref, mate_ref)):
        ids = ids_ref[:, ids_ref.shape[1] - LANES :].astype(jnp.float32)
        spread = route_matrix(ids, chips, per_device, active).astype(jnp.bfloat16)
        for j in range(0, half, WIDTH):
            back = jnp.concatenate([ref[s * SUB : (s + 1) * SUB, j : j + WIDTH] for ref in back_refs], axis=0)
            part = jnp.dot(spread, back, preferred_element_type=jnp.float32)
            out_refs[s][:, j : j + WIDTH] = part.astype(jnp.bfloat16)


def pair_kernel(kept_ref, received_ref, *refs, places):
    for k, out_ref in zip(places, refs[-len(places) :], strict=True):
        for s, ref in enumerate((kept_ref, received_ref)):
            out_ref[s * SUB : (s + 1) * SUB, :] = ref[k * SUB : (k + 1) * SUB, :]


def plan_kernel(active_ref, order_ref, out_ref, *, rows, nodes, near_rows, per_device):
    requests, active = active_ref.shape
    me = lax.axis_index("neuron")

    def match(cols):
        shape = (2 * rows, cols)
        item, slot = iota(shape, 0), iota(shape, 1)
        return item % rows // nodes, slot // SUB, slot % SUB == item // rows * nodes + item % nodes

    request, place, aligned = match(near_rows)
    device = 2 * (me // 2 ^ place // 2) + (me + place) % 2
    touched = jnp.zeros(aligned.shape, jnp.bool_)
    for r in range(requests):
        for a in range(active):
            touched = touched | ((request == r) & (device == active_ref[r, a] // per_device))
    near = jnp.where(touched & aligned, 1.0, 0.0)
    request, place, aligned = match(out_ref.shape[1] - near_rows)
    far = jnp.where((request == place) & aligned, 1.0, 0.0)
    out_ref[...] = jnp.concatenate([near, far], axis=1).astype(jnp.bfloat16)


def finish_kernel(plan_ref, *refs):
    part_refs, (tokens_ref, b_out_ref, out_ref) = refs[:-3], refs[-3:]
    rows, features = tokens_ref.shape
    half = features // 2
    plan = plan_ref[...]
    for j in range(0, half, WIDTH):
        parts = jnp.concatenate([ref[:, j : j + WIDTH] for ref in part_refs], axis=0)
        both = jnp.dot(plan, parts, preferred_element_type=jnp.float32)
        for h in range(2):
            at = h * half + j
            mixed = (
                tokens_ref[:, at : at + WIDTH].astype(jnp.float32)
                + both[h * rows : (h + 1) * rows]
                + b_out_ref[at : at + WIDTH].astype(jnp.float32).reshape(1, WIDTH)
            )
            out_ref[:, at : at + WIDTH] = mixed.astype(jnp.bfloat16)


def body(tokens, active, ln_gain, ln_bias, w_in, b_in, w_out, b_out):
    rows, features = tokens.shape
    requests, active_count = active.shape
    nodes = rows // requests
    units = w_in.shape[1]
    half = features // 2
    device_count = lax.axis_size("neuron")
    half_count = device_count // 2
    per_device = units // BLK
    packed = requests * SUB
    smem = pl.BlockSpec(memory_space=pltpu.SMEM)
    vmem = pl.BlockSpec(memory_space=pltpu.VMEM)
    hbm = pl.BlockSpec(memory_space=pl.ANY)
    chips = half_count // 2
    routing = dict(chips=chips, per_device=per_device, active=active_count)

    def call(kernel, shapes, in_specs, *operands, scratch=(), cost=0, limit=0):
        size = 2 * sum(rows * columns for rows, columns in shapes) + sum(x.size * 2 for x in operands)
        size += sum(2 * rows * columns for rows, columns in scratch)
        return pl.pallas_call(
            kernel,
            out_shape=[jax.ShapeDtypeStruct(shape, jnp.bfloat16) for shape in shapes],
            in_specs=in_specs,
            out_specs=[vmem] * len(shapes),
            scratch_shapes=[pltpu.VMEM(shape, jnp.bfloat16) for shape in scratch],
            compiler_params=pltpu.CompilerParams(vmem_limit_bytes=max(size + 8 * MIB, limit)),
            cost_estimate=pl.CostEstimate(flops=cost, bytes_accessed=size, transcendentals=0),
        )(*operands)

    def after(x, *others):
        return pl.pallas_call(
            lambda *refs: None,
            out_shape=jax.ShapeDtypeStruct(x.shape, x.dtype),
            in_specs=[hbm] * (1 + len(others)),
            out_specs=hbm,
            input_output_aliases={0: 0},
            compiler_params=pltpu.CompilerParams(vmem_limit_bytes=MIB),
            cost_estimate=pl.CostEstimate(flops=0, bytes_accessed=0, transcendentals=0),
        )(x, *others)

    def swap(x, partner):
        return lax.ppermute(x, "neuron", [(i, partner(i)) for i in range(device_count)])

    def across(x):
        return swap(x, lambda i: (i + half_count) % device_count)

    def mate_of(x):
        return swap(x, lambda i: i ^ 1)

    def to_chips(xs):
        return [xs[0]] + [swap(x, lambda i, k=k: i ^ 2 * k) for k, x in enumerate(xs) if k]

    def select(ids, packed_rows, order, cost):
        return call(
            functools.partial(select_kernel, **routing),
            [(2 * SUB, packed_rows[0].shape[1])] * chips,
            [vmem] * 4 + [hbm] * len(order),
            *ids, *packed_rows, *order,
            cost=cost,
        )

    def gather(ids, parts, order=()):
        back = to_chips(parts)
        return call(
            functools.partial(gather_kernel, **routing),
            [(packed, back[0].shape[1])] * 2,
            [vmem] * (2 + chips) + [hbm] * len(order),
            *ids, *back, *order,
        )

    [own] = call(
        functools.partial(norm_kernel, nodes=nodes),
        [(packed, half + LANES)],
        [smem, vmem, vmem, vmem],
        active, tokens, ln_gain, ln_bias,
        limit=56 * MIB,
    )
    other = across(own)
    near_ids = own, mate_of(own)
    near_rows = to_chips(select(near_ids, near_ids, (), 0))
    other = after(other, *near_rows[1:])
    far_ids = other, mate_of(other)
    far_rows = to_chips(select(far_ids, far_ids, (), SELECT_COST))
    parts = call(
        functools.partial(neuron_kernel, nodes=nodes, chips=chips),
        [(chips * SUB, half)] * 2 + [(2 * SUB, half)] * chips,
        [vmem] * (2 * chips + 3),
        *near_rows, *far_rows, w_in, b_in, w_out,
        scratch=[(2 * half_count * SUB, half + LANES)],
    )
    near_kept, near_received = parts[0], mate_of(parts[1])
    kept, passed = gather(far_ids, parts[2:])
    total = kept.astype(jnp.float32) + mate_of(passed).astype(jnp.float32)
    total = total.astype(jnp.bfloat16)

    def pair(places, order):
        return call(
            functools.partial(pair_kernel, places=places),
            [(2 * SUB, half)] * len(places),
            [vmem] * 2 + [hbm],
            near_kept, near_received, order,
        )

    split = range(2, chips)
    early = pair(split, passed)
    far_sum = across(total)
    late = pair(range(2), total)
    near_back = to_chips(late + early)
    near_count = 2 * SUB * chips
    [plan] = call(
        functools.partial(
            plan_kernel, rows=rows, nodes=nodes, near_rows=near_count, per_device=per_device
        ),
        [(2 * rows, near_count + packed)],
        [smem, hbm],
        active, total,
    )
    [mixed] = call(
        finish_kernel,
        [(rows, features)],
        [vmem] * (chips + 4),
        plan, *near_back, far_sum, tokens, b_out,
    )
    return mixed


def solution(mesh):
    placed = (
        P(("groups", "neuron"), None),
        P(("groups", "neuron"), None),
        P(),
        P(),
        P(None, "neuron"),
        P("neuron"),
        P("neuron", None),
        P(),
    )
    return jax.shard_map(
        body, mesh=mesh, in_specs=placed, out_specs=P(("groups", "neuron"), None), check_vma=False
    )
```

```python
import functools

import jax
import jax.numpy as jnp
from jax import lax
from jax.experimental import pallas as pl
from jax.experimental.pallas import tpu as pltpu
from jax.sharding import PartitionSpec as P

BLK = 128
LANES = 128
SUB = 8
WIDTH = 512
MIB = 1024 * 1024
SELECT_COST = 10_000_000_000

epsilon = 1e-05


def iota(shape, axis):
    return lax.broadcasted_iota(jnp.int32, shape, axis)


def touches(ids, device, per_device, active):
    owner = (ids.astype(jnp.int32) + (per_device - 1)) // per_device - 1
    touched = jnp.zeros(device.shape, jnp.bool_)
    for a in range(active):
        touched = touched | (owner[:, a : a + 1] == device)
    return touched


def route_matrix(ids, chips, per_device, active):
    shape = (ids.shape[0], chips * SUB)
    wanted = iota(shape, 1) % SUB == iota(shape, 0) % SUB
    me = lax.axis_index("neuron")
    device = 2 * (me // 2 ^ iota(shape, 1) // SUB) + me % 2
    return jnp.where(touches(ids, device, per_device, active) & wanted, 1.0, 0.0)


def norm_kernel(active_ref, tokens_ref, gain_ref, bias_ref, out_ref, *, nodes):
    rows, features = tokens_ref.shape
    half = features // 2
    packed = 2 * rows
    requests, active = active_ref.shape
    total = jnp.zeros((rows, WIDTH), jnp.float32)
    for j in range(0, features, WIDTH):
        total += tokens_ref[:, j : j + WIDTH].astype(jnp.float32)
    mean = jnp.sum(total, axis=1, keepdims=True) / features
    total = jnp.zeros((rows, WIDTH), jnp.float32)
    for j in range(0, features, WIDTH):
        centred = tokens_ref[:, j : j + WIDTH].astype(jnp.float32) - mean
        total += centred * centred
    scale = lax.rsqrt(jnp.sum(total, axis=1, keepdims=True) / features + epsilon)
    shape = (packed, packed)
    slot, item = iota(shape, 0), iota(shape, 1)
    source = (slot % SUB // nodes) * rows + slot // SUB * nodes + slot % nodes
    pack = jnp.where(item == source, 1.0, 0.0).astype(jnp.bfloat16)

    def normed(start):
        centred = tokens_ref[:, start : start + WIDTH].astype(jnp.float32) - mean
        gain = gain_ref[start : start + WIDTH].astype(jnp.float32).reshape(1, WIDTH)
        bias = bias_ref[start : start + WIDTH].astype(jnp.float32).reshape(1, WIDTH)
        return (centred * scale * gain + bias).astype(jnp.bfloat16)

    for j in range(0, half, WIDTH):
        both = jnp.concatenate([normed(j), normed(half + j)], axis=0)
        out_ref[:, j : j + WIDTH] = jnp.dot(pack, both, preferred_element_type=jnp.float32).astype(jnp.bfloat16)
    request, lane = iota((packed, LANES), 0) // SUB, iota((packed, LANES), 1)
    ids = jnp.zeros((packed, LANES), jnp.int32)
    for r in range(requests):
        for a in range(active):
            ids = jnp.where((request == r) & (lane == a), active_ref[r, a] + 1, ids)
    out_ref[:, half:] = ids.astype(jnp.float32).astype(jnp.bfloat16)


def select_kernel(own_ids_ref, mate_ids_ref, own_ref, mate_ref, *refs, chips, per_device, active):
    out_refs = refs[-chips:]
    total = own_ref.shape[1]
    for s, (ids_ref, packed_ref) in enumerate(((own_ids_ref, own_ref), (mate_ids_ref, mate_ref))):
        ids = ids_ref[:, ids_ref.shape[1] - LANES :].astype(jnp.float32)
        chosen = route_matrix(ids, chips, per_device, active).T.astype(jnp.bfloat16)
        for j in range(0, total, WIDTH):
            span = slice(j, min(j + WIDTH, total))
            rows = jnp.dot(chosen, packed_ref[:, span], preferred_element_type=jnp.float32)
            for k, out_ref in enumerate(out_refs):
                out_ref[s * SUB : (s + 1) * SUB, span] = rows[k * SUB : (k + 1) * SUB].astype(jnp.bfloat16)


def neuron_kernel(*refs, nodes, chips):
    x_ref = refs[-1]
    in_refs = [refs[:chips], refs[chips : 2 * chips]]
    at = 2 * chips
    w_in_ref, b_in_ref, w_out_ref = refs[at : at + 3]
    near_out_refs, far_out_refs = refs[at + 3 : at + 5], refs[at + 5 : -1]
    slots = x_ref.shape[0]
    features, units = w_in_ref.shape
    half = features // 2
    per_device = units // BLK
    depth = half // 4
    near_rows = 2 * SUB * chips
    for k in range(chips):
        here = slice(2 * SUB * k, 2 * SUB * (k + 1))
        x_ref[here, :] = in_refs[0][k][...]
        here = slice(near_rows + 2 * SUB * k, near_rows + 2 * SUB * (k + 1))
        x_ref[here, :] = in_refs[1][k][...]
    sums = []
    for h in range(2):
        total = jnp.zeros((slots, units), jnp.float32)
        for at in range(0, half, depth):
            total += jnp.dot(
                x_ref[:, at : at + depth],
                w_in_ref[h * half + at : h * half + at + depth, :],
                preferred_element_type=jnp.float32,
            )
        sums.append(total)
    first, second = sums
    upper = iota((slots, 1), 0) % SUB < nodes
    preact = jnp.where(
        upper,
        first + pltpu.roll(second, slots - nodes, 0),
        second + pltpu.roll(first, nodes, 0),
    ) + b_in_ref[...].astype(jnp.float32).reshape(1, units)
    ids = x_ref[:, half : half + LANES].astype(jnp.float32).astype(jnp.int32)
    own = lax.axis_index("neuron") * per_device + 1
    hidden = []
    for b in range(per_device):
        flag = jnp.max(jnp.where(ids == own + b, 1.0, 0.0), axis=1, keepdims=True)
        hidden.append(jnp.maximum(preact[:, b * BLK : (b + 1) * BLK], 0.0) * flag)
    hidden = jnp.concatenate(hidden, axis=1).astype(jnp.bfloat16)
    for at in range(0, half, depth):
        lo = jnp.dot(hidden, w_out_ref[:, at : at + depth], preferred_element_type=jnp.float32)
        hi = jnp.dot(hidden, w_out_ref[:, half + at : half + at + depth], preferred_element_type=jnp.float32)
        both = jnp.where(upper, lo, hi).astype(jnp.bfloat16)
        for k in range(chips):
            for s, near_out_ref in enumerate(near_out_refs):
                slot = both[(2 * k + s) * SUB : (2 * k + s + 1) * SUB]
                near_out_ref[k * SUB : (k + 1) * SUB, at : at + depth] = slot
            far = both[near_rows + 2 * SUB * k : near_rows + 2 * SUB * (k + 1)]
            far_out_refs[k][:, at : at + depth] = far


def gather_kernel(own_ref, mate_ref, *refs, chips, per_device, active):
    back_refs, out_refs = refs[:chips], refs[-2:]
    half = back_refs[0].shape[1]
    for s, ids_ref in enumerate((own_ref, mate_ref)):
        ids = ids_ref[:, ids_ref.shape[1] - LANES :].astype(jnp.float32)
        spread = route_matrix(ids, chips, per_device, active).astype(jnp.bfloat16)
        for j in range(0, half, WIDTH):
            back = jnp.concatenate([ref[s * SUB : (s + 1) * SUB, j : j + WIDTH] for ref in back_refs], axis=0)
            part = jnp.dot(spread, back, preferred_element_type=jnp.float32)
            out_refs[s][:, j : j + WIDTH] = part.astype(jnp.bfloat16)


def pair_kernel(kept_ref, received_ref, *refs, places):
    for k, out_ref in zip(places, refs[-len(places) :], strict=True):
        for s, ref in enumerate((kept_ref, received_ref)):
            out_ref[s * SUB : (s + 1) * SUB, :] = ref[k * SUB : (k + 1) * SUB, :]


def plan_kernel(active_ref, order_ref, out_ref, *, rows, nodes, near_rows, per_device):
    requests, active = active_ref.shape
    me = lax.axis_index("neuron")

    def match(cols):
        shape = (2 * rows, cols)
        item, slot = iota(shape, 0), iota(shape, 1)
        return item % rows // nodes, slot // SUB, slot % SUB == item // rows * nodes + item % nodes

    request, place, aligned = match(near_rows)
    device = 2 * (me // 2 ^ place // 2) + (me + place) % 2
    touched = jnp.zeros(aligned.shape, jnp.bool_)
    for r in range(requests):
        for a in range(active):
            touched = touched | ((request == r) & (device == active_ref[r, a] // per_device))
    near = jnp.where(touched & aligned, 1.0, 0.0)
    request, place, aligned = match(out_ref.shape[1] - near_rows)
    far = jnp.where((request == place) & aligned, 1.0, 0.0)
    out_ref[...] = jnp.concatenate([near, far], axis=1).astype(jnp.bfloat16)


def finish_kernel(plan_ref, *refs):
    part_refs, (tokens_ref, b_out_ref, out_ref) = refs[:-3], refs[-3:]
    rows, features = tokens_ref.shape
    half = features // 2
    plan = plan_ref[...]
    for j in range(0, half, WIDTH):
        parts = jnp.concatenate([ref[:, j : j + WIDTH] for ref in part_refs], axis=0)
        both = jnp.dot(plan, parts, preferred_element_type=jnp.float32)
        for h in range(2):
            at = h * half + j
            mixed = (
                tokens_ref[:, at : at + WIDTH].astype(jnp.float32)
                + both[h * rows : (h + 1) * rows]
                + b_out_ref[at : at + WIDTH].astype(jnp.float32).reshape(1, WIDTH)
            )
            out_ref[:, at : at + WIDTH] = mixed.astype(jnp.bfloat16)


def body(tokens, active, ln_gain, ln_bias, w_in, b_in, w_out, b_out):
    rows, features = tokens.shape
    requests, active_count = active.shape
    nodes = rows // requests
    units = w_in.shape[1]
    half = features // 2
    device_count = lax.axis_size("neuron")
    half_count = device_count // 2
    per_device = units // BLK
    packed = requests * SUB
    smem = pl.BlockSpec(memory_space=pltpu.SMEM)
    vmem = pl.BlockSpec(memory_space=pltpu.VMEM)
    hbm = pl.BlockSpec(memory_space=pl.ANY)
    chips = half_count // 2
    routing = dict(chips=chips, per_device=per_device, active=active_count)

    def call(kernel, shapes, in_specs, *operands, scratch=(), cost=0, limit=0):
        size = 2 * sum(rows * columns for rows, columns in shapes) + sum(x.size * 2 for x in operands)
        size += sum(2 * rows * columns for rows, columns in scratch)
        return pl.pallas_call(
            kernel,
            out_shape=[jax.ShapeDtypeStruct(shape, jnp.bfloat16) for shape in shapes],
            in_specs=in_specs,
            out_specs=[vmem] * len(shapes),
            scratch_shapes=[pltpu.VMEM(shape, jnp.bfloat16) for shape in scratch],
            compiler_params=pltpu.CompilerParams(vmem_limit_bytes=max(size + 8 * MIB, limit)),
            cost_estimate=pl.CostEstimate(flops=cost, bytes_accessed=size, transcendentals=0),
        )(*operands)

    def after(x, *others):
        return pl.pallas_call(
            lambda *refs: None,
            out_shape=jax.ShapeDtypeStruct(x.shape, x.dtype),
            in_specs=[hbm] * (1 + len(others)),
            out_specs=hbm,
            input_output_aliases={0: 0},
            compiler_params=pltpu.CompilerParams(vmem_limit_bytes=MIB),
            cost_estimate=pl.CostEstimate(flops=0, bytes_accessed=0, transcendentals=0),
        )(x, *others)

    def swap(x, partner):
        return lax.ppermute(x, "neuron", [(i, partner(i)) for i in range(device_count)])

    def across(x):
        return swap(x, lambda i: (i + half_count) % device_count)

    def mate_of(x):
        return swap(x, lambda i: i ^ 1)

    def to_chips(xs):
        return [xs[0]] + [swap(x, lambda i, k=k: i ^ 2 * k) for k, x in enumerate(xs) if k]

    def select(ids, packed_rows, order, cost):
        return call(
            functools.partial(select_kernel, **routing),
            [(2 * SUB, packed_rows[0].shape[1])] * chips,
            [vmem] * 4 + [hbm] * len(order),
            *ids, *packed_rows, *order,
            cost=cost,
        )

    def gather(ids, parts, order=()):
        back = to_chips(parts)
        return call(
            functools.partial(gather_kernel, **routing),
            [(packed, back[0].shape[1])] * 2,
            [vmem] * (2 + chips) + [hbm] * len(order),
            *ids, *back, *order,
        )

    [own] = call(
        functools.partial(norm_kernel, nodes=nodes),
        [(packed, half + LANES)],
        [smem, vmem, vmem, vmem],
        active, tokens, ln_gain, ln_bias,
        limit=56 * MIB,
    )
    other = across(own)
    near_ids = own, mate_of(own)
    near_rows = to_chips(select(near_ids, near_ids, (), 0))
    other = after(other, *near_rows[1:])
    far_ids = other, mate_of(other)
    far_rows = to_chips(select(far_ids, far_ids, (), SELECT_COST))
    parts = call(
        functools.partial(neuron_kernel, nodes=nodes, chips=chips),
        [(chips * SUB, half)] * 2 + [(2 * SUB, half)] * chips,
        [vmem] * (2 * chips + 3),
        *near_rows, *far_rows, w_in, b_in, w_out,
        scratch=[(2 * half_count * SUB, half + LANES)],
    )
    near_kept, near_received = parts[0], mate_of(parts[1])
    kept, passed = gather(far_ids, parts[2:])
    total = kept.astype(jnp.float32) + mate_of(passed).astype(jnp.float32)
    total = total.astype(jnp.bfloat16)

    def pair(places, order):
        return call(
            functools.partial(pair_kernel, places=places),
            [(2 * SUB, half)] * len(places),
            [vmem] * 2 + [hbm],
            near_kept, near_received, order,
        )

    split = range(2, chips)
    early = pair(split, passed)
    total = after(total, *early)
    far_sum = across(total)
    late = pair(range(2), total)
    near_back = to_chips(late + early)
    near_count = 2 * SUB * chips
    [plan] = call(
        functools.partial(
            plan_kernel, rows=rows, nodes=nodes, near_rows=near_count, per_device=per_device
        ),
        [(2 * rows, near_count + packed)],
        [smem, hbm],
        active, total,
    )
    [mixed] = call(
        finish_kernel,
        [(rows, features)],
        [vmem] * (chips + 4),
        plan, *near_back, far_sum, tokens, b_out,
    )
    return mixed


def solution(mesh):
    placed = (
        P(("groups", "neuron"), None),
        P(("groups", "neuron"), None),
        P(),
        P(),
        P(None, "neuron"),
        P("neuron"),
        P("neuron", None),
        P(),
    )
    return jax.shard_map(
        body, mesh=mesh, in_specs=placed, out_specs=P(("groups", "neuron"), None), check_vma=False
    )
```
